32 devices in a mesh: section: 4 (over z), shard: 8 (over y, x, core).
Axes of the slice: x: 2, y: 2, z: 4, core: 2. Of those that a mesh axis runs over, the one named last changes fastest.
Arguments:
- tokens: bfloat16 [4, 16, 8192], P(None, 'shard'), may hold values from -6 to 6
- lengths: int32 [4], replicated, may hold values from 1 to 16, 40 in all
- norm_gain: float32 [4, 8192], P('section'), may hold values from 0.25 to 1.75
- gate_tiles: bfloat16 [4, 128, 28, 128, 128], P('section', 'shard'), may hold values from -0.09375 to 0.09375
- up_tiles: bfloat16 [4, 128, 28, 128, 128], P('section', 'shard'), may hold values from -0.09375 to 0.09375
- in_index: int32 [4, 128, 28], P('section', 'shard'), may hold values from -1 to 63, as said below
- down_tiles: bfloat16 [4, 128, 28, 128, 128], P('section', 'shard'), may hold values from -0.0625 to 0.0625
- out_index: int32 [4, 128, 28], P('section', 'shard'), may hold values from -1 to 63, as said below
Outputs:
- hidden_states: bfloat16 [4, 4, 16, 8192], P('section', None, 'shard')
The draws below stay inside these ranges and needn't reach their ends.
Inputs may be any that keep to these rules, and one draw needn't show every extreme that they name: `in_index`: each list of 28 slots holds distinct block numbers first and -1 in the slots after them; at least 21 slots of every list hold a block number, and in each layer some list holds 28. `out_index`: each list of 28 slots holds distinct block numbers first and -1 in the slots after them; at least 21 slots of every list hold a block number, and in each layer some list holds 28.
All inputs are finite; a program needn't handle non-finite values.
Results may differ from the reference program's by a relative error of at most 0.035.
Values may be sent and summed in bfloat16 or wider, within the bound.
No kernel may reach another device: no remote copies, remote signals or barrier semaphores. Data moves between devices by JAX's collectives and lax.ppermute only.
A program may use at most 192 MiB of HBM per device.

```python
import math
import jax
import jax.numpy as jnp
import numpy as np
from jax import lax

D = 8192
FF = 16384
BLOCK = 128
KMAX = 28
MICRO = 4
NB = 64
FF_BLOCKS = 128
HB = 16
LAYERS = 4
ROWS_MB = 16
TOTAL_LIVE = 40
N_SHARD = 8


def block_lists(key):
    key_order, key_count, key_full = jax.random.split(key, 3)
    scores = jax.random.randint(key_order, (LAYERS, FF_BLOCKS, NB), 0, 1 << 20) * NB + jnp.arange(NB, dtype=jnp.int32)
    order = jnp.argsort(scores, axis=-1)[..., :KMAX].astype(jnp.int32)
    counts = jax.random.randint(key_count, (LAYERS, FF_BLOCKS), KMAX - KMAX // 4, KMAX + 1)
    full_group = jax.random.randint(key_full, (LAYERS,), 0, FF_BLOCKS)
    counts = jnp.where(jnp.arange(FF_BLOCKS)[None, :] == full_group[:, None], KMAX, counts)
    slot_ids = jnp.arange(KMAX, dtype=jnp.int32)
    return jnp.where(slot_ids[None, None, :] < counts[:, :, None], order, -1).astype(jnp.int32)


def draw_in_index(key, part):
    return block_lists(jax.random.fold_in(key, 11))


def draw_out_index(key, part):
    return block_lists(jax.random.fold_in(key, 23))


def block_levels(own_key, shape, cuts, low, high):
    gain, own = 1.0, jax.random.fold_in(own_key, 6)
    for axis_at, blocks in cuts:
        draws = jnp.exp(jax.random.uniform(jax.random.fold_in(own, axis_at), (blocks,), jnp.float32, low / len(cuts), high / len(cuts)))
        gain = gain * jnp.repeat(draws, shape[axis_at] // blocks).reshape([-1 if axis == axis_at else 1 for axis in range(len(shape))])
    return gain


def split_up(count, total, most, lean):
    portions = [(1 << 20) // math.isqrt(standing ** lean) + 1 for standing in range(2, count + 1)]
    spare, holding = total - most - (count - 1), [1] * (count - 1)
    while spare > 0:
        candidates = [i for i in range(count - 1) if holding[i] < most]
        pool, budget = sum([portions[i] for i in candidates]), spare
        for i in candidates:
            addition = min(most - holding[i], max(1, budget * portions[i] // pool), spare)
            holding[i] = holding[i] + addition
            spare = spare - addition
    return np.array([most] + holding)


def ragged_sizes(own_key, count, total, bound, slope):
    if count == 2:
        one = jax.random.randint(own_key, (), max(1, total - bound), min(bound, total - 1) + 1)
        return jnp.stack([one, total - one])
    sizes = jnp.asarray(split_up(count, total, bound, slope), jnp.int32)
    twos = (count - 1) // 2
    source_of, receiver = sizes[1:1 + 2 * twos:2], sizes[2:2 + 2 * twos:2]
    slack = jnp.minimum(source_of - 1, bound - receiver)
    shifted = jax.random.randint(jax.random.fold_in(own_key, 1), (twos,), 0, 1 << 20) % (slack + 1)
    sizes = sizes.at[1:1 + 2 * twos:2].set(source_of - shifted).at[2:2 + 2 * twos:2].set(receiver + shifted)
    return sizes[jax.random.permutation(jax.random.fold_in(own_key, 2), count)]


def gaussian(stream_key, shape, scale, reach, cuts=(), kind=jnp.bfloat16):
    array = scale * jax.random.normal(stream_key, shape, jnp.float32)
    if cuts:
        array = array * block_levels(stream_key, shape, cuts, -0.22, 0.18)
    return jnp.clip(array, -reach, reach).astype(kind)


def setup_inputs(seed: int = 0) -> dict:
    arg_keys = jax.random.split(jax.random.key(seed), 9)
    tokens = gaussian(arg_keys[0], (MICRO, ROWS_MB, D), 1.0, 6.0, ((1, 8),))
    lengths = ragged_sizes(arg_keys[1], MICRO, TOTAL_LIVE, ROWS_MB, 1).astype(jnp.int32)
    norm_gain = jnp.clip(1.0 + 0.15 * jax.random.normal(arg_keys[2], (LAYERS, D), jnp.float32), 0.25, 1.75)
    gate_tiles = gaussian(arg_keys[3], (LAYERS, FF_BLOCKS, KMAX, BLOCK, BLOCK), (KMAX * BLOCK) ** -0.5, 0.09375, ((0, 4), (1, 8)))
    up_tiles = gaussian(arg_keys[4], (LAYERS, FF_BLOCKS, KMAX, BLOCK, BLOCK), (KMAX * BLOCK) ** -0.5, 0.09375, ((0, 4), (1, 8)))
    in_index = draw_in_index(jax.random.fold_in(arg_keys[8], 71), 0)
    down_tiles = gaussian(arg_keys[6], (LAYERS, FF_BLOCKS, KMAX, BLOCK, BLOCK), (FF * KMAX // NB) ** -0.5, 0.0625, ((0, 4), (1, 8)))
    out_index = draw_out_index(jax.random.fold_in(arg_keys[8], 71), 0)
    return {"tokens": tokens, "lengths": lengths, "norm_gain": norm_gain, "gate_tiles": gate_tiles, "up_tiles": up_tiles, "in_index": in_index, "down_tiles": down_tiles, "out_index": out_index}


norm_eps = 1e-05

def group_terms(normed, gate_group, up_group, in_group, down_group, out_group):
    row_count = normed.shape[0]
    column_blocks = normed.reshape(row_count, NB, BLOCK)
    in_valid = (in_group >= 0).astype(jnp.bfloat16)
    picked = jnp.take(column_blocks, jnp.maximum(in_group, 0).astype(jnp.int32), axis=1)
    picked = picked * in_valid[None, :, :, None]
    picked = picked.astype(jnp.float32)
    gate_val = jnp.einsum('nhkc,hkcf->nhf', picked, gate_group.astype(jnp.float32), precision=lax.Precision.HIGHEST)
    up_val = jnp.einsum('nhkc,hkcf->nhf', picked, up_group.astype(jnp.float32), precision=lax.Precision.HIGHEST)
    hidden = (jax.nn.silu(gate_val) * up_val).astype(jnp.bfloat16)
    part_terms = jnp.einsum('nhc,hkcf->nhkf', hidden.astype(jnp.float32), down_group.astype(jnp.float32), precision=lax.Precision.HIGHEST)
    onehot = (out_group[:, :, None] == jnp.arange(NB, dtype=jnp.int32)[None, None, :]).astype(jnp.float32)
    placed = jnp.einsum('nhkf,hkb->nbf', part_terms, onehot, precision=lax.Precision.HIGHEST)
    return placed.reshape(row_count, D).astype(jnp.bfloat16)

def layer_apply(arrived, keep_row, gain_row, gate_layer, up_layer, in_layer, down_layer, out_layer):
    widened = arrived.astype(jnp.float32)
    scale_row = lax.rsqrt(lax.optimization_barrier(jnp.mean(widened * widened, axis=-1, keepdims=True)) + norm_eps)
    normed = (widened * scale_row * gain_row[None, :]).astype(jnp.bfloat16)
    grouped = (gate_layer.reshape(N_SHARD, HB, KMAX, BLOCK, BLOCK), up_layer.reshape(N_SHARD, HB, KMAX, BLOCK, BLOCK), in_layer.reshape(N_SHARD, HB, KMAX), down_layer.reshape(N_SHARD, HB, KMAX, BLOCK, BLOCK), out_layer.reshape(N_SHARD, HB, KMAX))

    def accumulate(summed, group):
        term = group_terms(normed, group[0], group[1], group[2], group[3], group[4])
        return (summed + term.astype(jnp.float32), None)
    summed, _ = lax.scan(accumulate, jnp.zeros(widened.shape, jnp.float32), grouped)
    return jnp.where(keep_row[:, None], widened + summed, jnp.float32(0.0)).astype(jnp.bfloat16)

def reference(tokens, lengths, norm_gain, gate_tiles, up_tiles, in_index, down_tiles, out_index):
    row_ids = jnp.arange(ROWS_MB, dtype=jnp.int32)
    keep_all = (row_ids[None, :] < lengths[:, None]).reshape(MICRO * ROWS_MB)
    current = tokens.reshape(MICRO * ROWS_MB, D)
    results = []
    for layer_id in range(LAYERS):
        current = layer_apply(current, keep_all, norm_gain[layer_id], gate_tiles[layer_id], up_tiles[layer_id], in_index[layer_id], down_tiles[layer_id], out_index[layer_id])
        results.append(current.reshape(MICRO, ROWS_MB, D))
    return jnp.stack(results, axis=0)
```

```python
import functools

import jax
import jax.numpy as jnp
from jax import lax
from jax.experimental import pallas as pl
from jax.experimental.pallas import tpu as pltpu
from jax.sharding import PartitionSpec as P

norm_eps = 1e-05
f32 = jnp.float32
bf16 = jnp.bfloat16
MIB = 2**20
VMEM_SPEC = pl.BlockSpec(memory_space=pltpu.VMEM)
SMEM_SPEC = pl.BlockSpec(memory_space=pltpu.SMEM)
ANY_SPEC = pl.BlockSpec(memory_space=pl.ANY)


def live_total(tokens_shape, shard_total):
    micro_count, own_count, _ = tokens_shape
    return micro_count * own_count * shard_total * 5 // 8


def xor_shard(value, mask):
    size = lax.axis_size("shard")
    return lax.ppermute(value, "shard", [(i, i ^ mask) for i in range(size)])


def spread(value):
    size = lax.axis_size("shard")
    same_core = [value] + [xor_shard(value, mask) for mask in range(2, size, 2)]
    other_core = [xor_shard(part, 1) for part in same_core]
    return [part for pair in zip(same_core, other_core) for part in pair]


def vmem_limit(rows):
    return (12 if rows <= 64 else 32) * MIB


def in_vmem(value):
    return pltpu.with_memory_space_constraint(value, pltpu.VMEM)


def load_kernel(info_ref, gate_ref, up_ref, down_ref, held_ref, sems):
    blocks = gate_ref.shape[0]

    def copies(h):
        return [
            pltpu.make_async_copy(ref.at[h], held_ref.at[i, h], sems.at[i, h])
            for i, ref in enumerate((gate_ref, up_ref, down_ref))
        ]

    @pl.loop(0, blocks)
    def _(h):
        for copy in copies(h):
            copy.start()

    @pl.loop(0, blocks)
    def _(h):
        for copy in copies(h):
            copy.wait()


def load_weights(info, gate, up, down, rows):
    shape = (3,) + gate.shape
    size = gate.size * 3
    return pl.pallas_call(
        load_kernel,
        out_shape=pltpu.VMEM(shape, bf16),
        in_specs=[SMEM_SPEC] + [ANY_SPEC] * 3,
        out_specs=VMEM_SPEC,
        scratch_shapes=[pltpu.SemaphoreType.DMA((3, gate.shape[0]))],
        compiler_params=pltpu.CompilerParams(vmem_limit_bytes=vmem_limit(rows) + 0 * MIB),
        cost_estimate=pl.CostEstimate(flops=0, bytes_accessed=size * 2, transcendentals=0),
        name="load_weights",
    )(info, gate, up, down)


def row_starts(lengths_ref, micro_count):
    starts = [jnp.int32(0)]
    for m in range(micro_count):
        starts.append(starts[-1] + lengths_ref[m])
    return starts


def layer_kernel(first, rows, unroll, shard_total, micro_count, own_count, *refs):
    info_ref, lengths_ref, in_ref, out_ref, gain_ref, held_ref = refs[:6]
    rest = list(refs[6:])
    shard_id = info_ref[0]
    blocks, slots, block = held_ref.shape[1], held_ref.shape[2], held_ref.shape[4]
    block_total = gain_ref.shape[0]
    chunk_blocks = block_total // shard_total
    chunks = [rest.pop(0) for _ in range(shard_total)]
    even_ref, odd_ref = rest.pop(0), rest.pop(0)
    own_ref = rest.pop(0) if first else None
    normed, hidden, total = rest

    squares = jnp.zeros((rows, block), f32)
    if first:
        starts = row_starts(lengths_ref, micro_count)
        group = micro_count * own_count
        place = lax.broadcasted_iota(jnp.int32, (rows, group), 0)
        local = lax.broadcasted_iota(jnp.int32, (rows, group), 1)
        picks = []
        for j in range(shard_total):
            device = shard_id ^ j
            target = jnp.full((rows, group), -1, jnp.int32)
            for m in range(micro_count):
                for q in range(own_count):
                    row = device * own_count + q
                    to = jnp.where(row < lengths_ref[m], starts[m] + row, -1)
                    target = jnp.where(local == m * own_count + q, to, target)
            picks.append((target == place).astype(f32))
        pick = jnp.concatenate(picks, axis=1).astype(bf16)
        for c in range(shard_total):
            columns = pl.ds(c * chunk_blocks * block, chunk_blocks * block)
            spans = jnp.concatenate([ref[:, columns].astype(f32) for ref in chunks], axis=0)
            raw = jnp.dot(pick, spans.astype(bf16), preferred_element_type=f32)
            for i in range(chunk_blocks):
                piece = raw[:, i * block : (i + 1) * block]
                squares += piece * piece
                normed[c * chunk_blocks + i] = piece.astype(bf16)
        for i in range(chunk_blocks):
            own_ref[:, i * block : (i + 1) * block] = normed[shard_id * chunk_blocks + i]
    else:
        for j in range(shard_total):
            base = (shard_id ^ j) * chunk_blocks
            for i in range(chunk_blocks):
                piece = chunks[j][:, i * block : (i + 1) * block]
                normed[base + i] = piece
                wide = piece.astype(f32)
                squares += wide * wide
    mean = jnp.sum(squares, axis=1, keepdims=True) / (block_total * block)
    scale = lax.rsqrt(mean + norm_eps)
    for b in range(block_total):
        normed[b] = (normed[b].astype(f32) * scale * gain_ref[b : b + 1, :]).astype(bf16)
    normed[block_total] = jnp.zeros((rows, block), bf16)
    total[...] = jnp.zeros_like(total)

    def at(ref, h, k):
        index = ref[h, k]
        return jnp.where(index < 0, block_total, index)

    @pl.loop(0, blocks // unroll)
    def _(step):
        for q in range(unroll):
            h = step * unroll + q
            picked = jnp.concatenate([normed[at(in_ref, h, k)] for k in range(slots)], axis=1)
            gate = jnp.dot(
                picked, held_ref[0, h].reshape(slots * block, block), preferred_element_type=f32
            )
            up = jnp.dot(
                picked, held_ref[1, h].reshape(slots * block, block), preferred_element_type=f32
            )
            hidden[h] = (gate / (1.0 + jnp.exp(-gate)) * up).astype(bf16)

    @pl.loop(0, blocks // unroll)
    def _(step):
        for q in range(unroll):
            h = step * unroll + q
            rows_in = hidden[h]
            for k in range(0, slots, 2):
                pair = jnp.concatenate([held_ref[2, h, k], held_ref[2, h, k + 1]], axis=1)
                product = jnp.dot(rows_in, pair, preferred_element_type=f32)
                for p in range(2):
                    total[at(out_ref, h, k + p)] += product[:, p * block : (p + 1) * block]

    for j in range(shard_total):
        base = (shard_id ^ j) * chunk_blocks
        target = (odd_ref if j % 2 else even_ref).at[j // 2]
        for i in range(chunk_blocks):
            target[:, i * block : (i + 1) * block] = total[base + i].astype(bf16)


def layer_step(first, rows, info, lengths, in_index, out_index, gain, held, chunks, micro_count, own_count):
    shard_total = len(chunks)
    _, blocks, slots, block, _ = held.shape
    block_total = gain.shape[0]
    width = block_total * block // shard_total
    unroll = 2 if blocks % 2 == 0 else 1
    outs = [pltpu.VMEM((shard_total // 2, rows, width), bf16)] * 2
    if first:
        outs.append(pltpu.VMEM((rows, width), bf16))
    return pl.pallas_call(
        functools.partial(layer_kernel, first, rows, unroll, shard_total, micro_count, own_count),
        out_shape=outs,
        in_specs=[SMEM_SPEC] * 4 + [VMEM_SPEC] * (2 + shard_total),
        out_specs=[VMEM_SPEC] * len(outs),
        scratch_shapes=[
            pltpu.VMEM((block_total + 1, rows, block), bf16),
            pltpu.VMEM((blocks, rows, block), bf16),
            pltpu.VMEM((block_total + 1, rows, block), f32),
        ],
        compiler_params=pltpu.CompilerParams(vmem_limit_bytes=vmem_limit(rows)),
        cost_estimate=pl.CostEstimate(
            flops=2 * rows * held.size, bytes_accessed=0, transcendentals=0
        ),
        name="layer_first" if first else "layer",
    )(info, lengths, in_index, out_index, gain, held, *map(in_vmem, chunks))


def pair_kernel(held_ref, even_ref, came_ref, own_ref, *send_refs):
    own_ref[...] = even_ref[0].astype(f32) + came_ref[0].astype(f32)
    for i, ref in enumerate(send_refs):
        ref[...] = (even_ref[i + 1].astype(f32) + came_ref[i + 1].astype(f32)).astype(bf16)


def pair_sum(held, even, came):
    parts, rows, width = even.shape
    return pl.pallas_call(
        pair_kernel,
        out_shape=[pltpu.VMEM((rows, width), f32)] + [pltpu.VMEM((rows, width), bf16)] * (parts - 1),
        in_specs=[VMEM_SPEC] * 3,
        out_specs=[VMEM_SPEC] * parts,
        compiler_params=pltpu.CompilerParams(vmem_limit_bytes=vmem_limit(rows)),
        name="pair_sum",
    )(held, in_vmem(even), in_vmem(came))


def finish_kernel(turn, info_ref, held_ref, x_ref, own_ref, *refs):
    fresh_ref, kept_out_ref = refs[-2:]
    sum_value = own_ref[...]
    for ref in refs[:-3]:
        sum_value = sum_value + ref[...].astype(f32)
    fresh = (x_ref[...].astype(f32) + sum_value).astype(bf16)
    fresh_ref[...] = fresh
    kept_ref = refs[-3]
    kept_out_ref[...] = jnp.where(info_ref[1] == turn, fresh, kept_ref[...])


def finish_sum(turn, info, held, x_own, own, came, kept):
    rows, width = x_own.shape
    return pl.pallas_call(
        functools.partial(finish_kernel, turn),
        out_shape=[pltpu.VMEM((rows, width), bf16)] * 2,
        in_specs=[SMEM_SPEC] + [VMEM_SPEC] * (4 + len(came)),
        out_specs=[VMEM_SPEC] * 2,
        compiler_params=pltpu.CompilerParams(vmem_limit_bytes=vmem_limit(rows)),
        name="finish_sum",
    )(info, held, *map(in_vmem, (x_own, own, *came, kept)))


def result_kernel(info_ref, lengths_ref, *refs):
    chunks, out_ref = refs[:-1], refs[-1]
    micro_count, own_count, _ = out_ref.shape
    shard_id = info_ref[0]
    rows, width = chunks[0].shape
    starts = row_starts(lengths_ref, micro_count)
    group = micro_count * own_count
    place = lax.broadcasted_iota(jnp.int32, (group, rows), 1)
    local = lax.broadcasted_iota(jnp.int32, (group, rows), 0)
    target = jnp.full((group, rows), -1, jnp.int32)
    for m in range(micro_count):
        for q in range(own_count):
            row = shard_id * own_count + q
            to = jnp.where(row < lengths_ref[m], starts[m] + row, -1)
            target = jnp.where(local == m * own_count + q, to, target)
    pick = (target == place).astype(f32).astype(bf16)
    for j, ref in enumerate(chunks):
        columns = pl.ds(pl.multiple_of((shard_id ^ j) * width, width), width)
        value = jnp.dot(pick, ref[...], preferred_element_type=f32)
        for m in range(micro_count):
            out_ref[m, :, columns] = value[m * own_count : (m + 1) * own_count].astype(bf16)


def result_rows(info, lengths, chunks, shape):
    rows = chunks[0].shape[0]
    return pl.pallas_call(
        result_kernel,
        out_shape=jax.ShapeDtypeStruct(shape, bf16),
        in_specs=[SMEM_SPEC] * 2 + [VMEM_SPEC] * len(chunks),
        out_specs=VMEM_SPEC,
        compiler_params=pltpu.CompilerParams(vmem_limit_bytes=vmem_limit(rows)),
        name="result_rows",
    )(info, lengths, *map(in_vmem, chunks))


def body(tokens, lengths, norm_gain, gate_tiles, up_tiles, in_index, down_tiles, out_index):
    micro_count, own_count, model_width = tokens.shape
    block = gate_tiles.shape[-1]
    section_id = lax.axis_index("section")
    section_total = lax.axis_size("section")
    shard_total = lax.axis_size("shard")
    rows = live_total(tokens.shape, shard_total)
    info = jnp.stack([lax.axis_index("shard"), section_id])
    gain = norm_gain.reshape(model_width // block, block)
    held = load_weights(info, gate_tiles[0], up_tiles[0], down_tiles[0], rows)
    held = in_vmem(held)
    chunks = spread(tokens.reshape(micro_count * own_count, model_width))
    for turn in range(section_total):
        first = turn == 0
        parts = layer_step(
            first, rows, info, lengths, in_index[0], out_index[0], gain, held, chunks, micro_count, own_count
        )
        x_own = parts[2] if first else chunks[0]
        sums = pair_sum(held, parts[0], xor_shard(parts[1], 1))
        came = [xor_shard(part, 2 * i + 2) for i, part in enumerate(sums[1:])]
        kept = x_own if first else kept
        fresh, kept = finish_sum(turn, info, held, x_own, sums[0], came, kept)
        if turn + 1 < section_total:
            moved = lax.ppermute(
                fresh, "section", [(i, i + 1) for i in range(section_total - 1)]
            )
            chunks = spread(moved)
    return result_rows(info, lengths, spread(kept), tokens.shape)[None]


def solution(mesh):
    placed = (
        P(None, "shard", None),
        P(),
        P("section", None),
        P("section", "shard", None, None, None),
        P("section", "shard", None, None, None),
        P("section", "shard", None),
        P("section", "shard", None, None, None),
        P("section", "shard", None),
    )
    return jax.shard_map(
        body,
        mesh=mesh,
        in_specs=placed,
        out_specs=P("section", None, "shard", None),
        check_vma=False,
    )
```

```python
import functools

import jax
import jax.numpy as jnp
from jax import lax
from jax.experimental import pallas as pl
from jax.experimental.pallas import tpu as pltpu
from jax.sharding import PartitionSpec as P

norm_eps = 1e-05
f32 = jnp.float32
bf16 = jnp.bfloat16
MIB = 2**20
UNROLL = 4
VMEM_SPEC = pl.BlockSpec(memory_space=pltpu.VMEM)
SMEM_SPEC = pl.BlockSpec(memory_space=pltpu.SMEM)
ANY_SPEC = pl.BlockSpec(memory_space=pl.ANY)


def live_total(tokens_shape, shard_total):
    micro_count, own_count, _ = tokens_shape
    return micro_count * own_count * shard_total * 5 // 8


def xor_shard(value, mask):
    size = lax.axis_size("shard")
    return lax.ppermute(value, "shard", [(i, i ^ mask) for i in range(size)])


def same_core(value):
    size = lax.axis_size("shard")
    return [value] + [xor_shard(value, mask) for mask in range(2, size, 2)]


def next_section(value, turn):
    size = lax.axis_size("shard")
    start = turn * size
    return [
        lax.ppermute(
            value,
            ("section", "shard"),
            [(start + i, start + size + (i ^ mask)) for i in range(size)],
        )
        for mask in range(0, size, 2)
    ]


def both_cores(parts):
    other_core = [xor_shard(part, 1) for part in parts]
    return [part for pair in zip(parts, other_core) for part in pair]


def vmem_limit(rows):
    return (12 if rows <= 64 else 32) * MIB


def in_vmem(value):
    return pltpu.with_memory_space_constraint(value, pltpu.VMEM)


def load_kernel(info_ref, gate_ref, up_ref, held_ref, sems):
    blocks = gate_ref.shape[0]

    def copies(h):
        return [
            pltpu.make_async_copy(ref.at[h], held_ref.at[i, h], sems.at[i, h])
            for i, ref in enumerate((gate_ref, up_ref))
        ]

    @pl.loop(0, blocks)
    def _(h):
        for copy in copies(h):
            copy.start()

    @pl.loop(0, blocks)
    def _(h):
        for copy in copies(h):
            copy.wait()


def load_weights(info, gate, up, rows):
    shape = (3,) + gate.shape
    size = gate.size * 2
    return pl.pallas_call(
        load_kernel,
        out_shape=pltpu.VMEM(shape, bf16),
        in_specs=[SMEM_SPEC] + [ANY_SPEC] * 2,
        out_specs=VMEM_SPEC,
        scratch_shapes=[pltpu.SemaphoreType.DMA((2, gate.shape[0]))],
        compiler_params=pltpu.CompilerParams(vmem_limit_bytes=vmem_limit(rows)),
        cost_estimate=pl.CostEstimate(flops=0, bytes_accessed=size * 2, transcendentals=0),
        name="load_weights",
    )(info, gate, up)


def relay_kernel(held_ref, *refs):
    half = len(refs) // 2
    for source, target in zip(refs[:half], refs[half:]):
        target[...] = source[...]


def relay(held, parts, rows):
    return pl.pallas_call(
        relay_kernel,
        out_shape=[pltpu.VMEM(part.shape, part.dtype) for part in parts],
        in_specs=[VMEM_SPEC] * (1 + len(parts)),
        out_specs=[VMEM_SPEC] * len(parts),
        compiler_params=pltpu.CompilerParams(vmem_limit_bytes=vmem_limit(rows)),
        name="relay",
    )(held, *map(in_vmem, parts))


def row_starts(lengths_ref, micro_count):
    starts = [jnp.int32(0)]
    for m in range(micro_count):
        starts.append(starts[-1] + lengths_ref[m])
    return starts


def layer_kernel(first, rows, unroll, shard_total, micro_count, own_count, *refs):
    info_ref, lengths_ref, in_ref, out_ref, gain_ref, held_ref = refs[:6]
    rest = list(refs[6:])
    down_ref = rest.pop(0) if first else None
    shard_id = info_ref[0]
    blocks, slots, block = held_ref.shape[1], held_ref.shape[2], held_ref.shape[4]
    block_total = gain_ref.shape[0]
    chunk_blocks = block_total // shard_total
    chunks = [rest.pop(0) for _ in range(shard_total)]
    even_ref, odd_ref = rest.pop(0), rest.pop(0)
    if first:
        own_ref, filled_ref = rest.pop(0), rest.pop(0)
        sems = rest.pop()

        def copy_down(h):
            return pltpu.make_async_copy(down_ref.at[h], filled_ref.at[2, h], sems.at[h])

        @pl.loop(0, blocks)
        def _(h):
            copy_down(h).start()
    else:
        filled_ref = held_ref
    normed, hidden, total = rest

    squares = jnp.zeros((rows, block), f32)
    if first:
        starts = row_starts(lengths_ref, micro_count)
        group = micro_count * own_count
        place = lax.broadcasted_iota(jnp.int32, (rows, group), 0)
        local = lax.broadcasted_iota(jnp.int32, (rows, group), 1)
        picks = []
        for j in range(shard_total):
            device = shard_id ^ j
            target = jnp.full((rows, group), -1, jnp.int32)
            for m in range(micro_count):
                for q in range(own_count):
                    row = device * own_count + q
                    to = jnp.where(row < lengths_ref[m], starts[m] + row, -1)
                    target = jnp.where(local == m * own_count + q, to, target)
            picks.append((target == place).astype(f32))
        pick = jnp.concatenate(picks, axis=1).astype(bf16)
        for c in range(shard_total):
            columns = pl.ds(c * chunk_blocks * block, chunk_blocks * block)
            spans = jnp.concatenate([ref[:, columns].astype(f32) for ref in chunks], axis=0)
            raw = jnp.dot(pick, spans.astype(bf16), preferred_element_type=f32)
            for i in range(chunk_blocks):
                piece = raw[:, i * block : (i + 1) * block]
                squares += piece * piece
                normed[c * chunk_blocks + i] = piece.astype(bf16)
        for i in range(chunk_blocks):
            own_ref[:, i * block : (i + 1) * block] = normed[shard_id * chunk_blocks + i]
    else:
        for j in range(shard_total):
            base = (shard_id ^ j) * chunk_blocks
            for i in range(chunk_blocks):
                piece = chunks[j][:, i * block : (i + 1) * block]
                normed[base + i] = piece
                wide = piece.astype(f32)
                squares += wide * wide
    mean = jnp.sum(squares, axis=1, keepdims=True) / (block_total * block)
    scale = lax.rsqrt(mean + norm_eps)
    for b in range(block_total):
        normed[b] = (normed[b].astype(f32) * scale * gain_ref[b : b + 1, :]).astype(bf16)
    normed[block_total] = jnp.zeros((rows, block), bf16)
    total[...] = jnp.zeros_like(total)

    def at(ref, h, k):
        index = ref[h, k]
        return jnp.where(index < 0, block_total, index)

    @pl.loop(0, blocks // unroll)
    def _(step):
        for q in range(unroll):
            h = step * unroll + q
            picked = jnp.concatenate([normed[at(in_ref, h, k)] for k in range(slots)], axis=1)
            gate = jnp.dot(
                picked, held_ref[0, h].reshape(slots * block, block), preferred_element_type=f32
            )
            up = jnp.dot(
                picked, held_ref[1, h].reshape(slots * block, block), preferred_element_type=f32
            )
            hidden[h] = (gate / (1.0 + jnp.exp(-gate)) * up).astype(bf16)

    @pl.loop(0, blocks // unroll)
    def _(step):
        for q in range(unroll):
            h = step * unroll + q
            if first:
                copy_down(h).wait()
            rows_in = hidden[h]
            for k in range(0, slots, 2):
                pair = jnp.concatenate([filled_ref[2, h, k], filled_ref[2, h, k + 1]], axis=1)
                product = jnp.dot(rows_in, pair, preferred_element_type=f32)
                for p in range(2):
                    total[at(out_ref, h, k + p)] += product[:, p * block : (p + 1) * block]

    for j in range(shard_total):
        base = (shard_id ^ j) * chunk_blocks
        target = (odd_ref if j % 2 else even_ref).at[j // 2]
        for i in range(chunk_blocks):
            target[:, i * block : (i + 1) * block] = total[base + i].astype(bf16)


def layer_step(first, rows, info, lengths, in_index, out_index, gain, held, down, chunks, micro_count, own_count):
    shard_total = len(chunks)
    _, blocks, slots, block, _ = held.shape
    block_total = gain.shape[0]
    width = block_total * block // shard_total
    unroll = max(u for u in (1, 2, UNROLL) if blocks % u == 0)
    outs = [pltpu.VMEM((shard_total // 2, rows, width), bf16)] * 2
    if first:
        outs.append(pltpu.VMEM((rows, width), bf16))
        outs.append(pltpu.VMEM(held.shape, bf16))
    return pl.pallas_call(
        functools.partial(layer_kernel, first, rows, unroll, shard_total, micro_count, own_count),
        out_shape=outs,
        in_specs=[SMEM_SPEC] * 4
        + [VMEM_SPEC] * 2
        + [ANY_SPEC] * first
        + [VMEM_SPEC] * shard_total,
        out_specs=[VMEM_SPEC] * len(outs),
        scratch_shapes=[
            pltpu.VMEM((block_total + 1, rows, block), bf16),
            pltpu.VMEM((blocks, rows, block), bf16),
            pltpu.VMEM((block_total + 1, rows, block), f32),
        ]
        + ([pltpu.SemaphoreType.DMA((blocks,))] if first else []),
        compiler_params=pltpu.CompilerParams(vmem_limit_bytes=vmem_limit(rows)),
        cost_estimate=pl.CostEstimate(
            flops=2 * rows * held.size, bytes_accessed=0, transcendentals=0
        ),
        input_output_aliases={5: 3} if first else {},
        name="layer_first" if first else "layer",
    )(info, lengths, in_index, out_index, gain, held, *([down] if first else []), *map(in_vmem, chunks))


def pair_kernel(held_ref, even_ref, came_ref, own_ref, *send_refs):
    own_ref[...] = even_ref[0].astype(f32) + came_ref[0].astype(f32)
    for i, ref in enumerate(send_refs):
        ref[...] = (even_ref[i + 1].astype(f32) + came_ref[i + 1].astype(f32)).astype(bf16)


def pair_sum(held, even, came):
    parts, rows, width = even.shape
    return pl.pallas_call(
        pair_kernel,
        out_shape=[pltpu.VMEM((rows, width), f32)] + [pltpu.VMEM((rows, width), bf16)] * (parts - 1),
        in_specs=[VMEM_SPEC] * 3,
        out_specs=[VMEM_SPEC] * parts,
        compiler_params=pltpu.CompilerParams(vmem_limit_bytes=vmem_limit(rows)),
        name="pair_sum",
    )(held, in_vmem(even), in_vmem(came))


def finish_kernel(turn, info_ref, held_ref, x_ref, own_ref, *refs):
    fresh_ref, kept_out_ref = refs[-2:]
    sum_value = own_ref[...]
    for ref in refs[:-3]:
        sum_value = sum_value + ref[...].astype(f32)
    fresh = (x_ref[...].astype(f32) + sum_value).astype(bf16)
    fresh_ref[...] = fresh
    kept_ref = refs[-3]
    kept_out_ref[...] = jnp.where(info_ref[1] == turn, fresh, kept_ref[...])


def finish_sum(turn, info, held, x_own, own, came, kept):
    rows, width = x_own.shape
    return pl.pallas_call(
        functools.partial(finish_kernel, turn),
        out_shape=[pltpu.VMEM((rows, width), bf16)] * 2,
        in_specs=[SMEM_SPEC] + [VMEM_SPEC] * (4 + len(came)),
        out_specs=[VMEM_SPEC] * 2,
        compiler_params=pltpu.CompilerParams(vmem_limit_bytes=vmem_limit(rows)),
        name="finish_sum",
    )(info, held, *map(in_vmem, (x_own, own, *came, kept)))


def result_kernel(info_ref, lengths_ref, *refs):
    chunks, out_ref = refs[:-1], refs[-1]
    micro_count, own_count, _ = out_ref.shape
    shard_id = info_ref[0]
    rows, width = chunks[0].shape
    starts = row_starts(lengths_ref, micro_count)
    group = micro_count * own_count
    place = lax.broadcasted_iota(jnp.int32, (group, rows), 1)
    local = lax.broadcasted_iota(jnp.int32, (group, rows), 0)
    target = jnp.full((group, rows), -1, jnp.int32)
    for m in range(micro_count):
        for q in range(own_count):
            row = shard_id * own_count + q
            to = jnp.where(row < lengths_ref[m], starts[m] + row, -1)
            target = jnp.where(local == m * own_count + q, to, target)
    pick = (target == place).astype(f32).astype(bf16)
    for j, ref in enumerate(chunks):
        columns = pl.ds(pl.multiple_of((shard_id ^ j) * width, width), width)
        value = jnp.dot(pick, ref[...], preferred_element_type=f32)
        for m in range(micro_count):
            out_ref[m, :, columns] = value[m * own_count : (m + 1) * own_count].astype(bf16)


def result_rows(info, lengths, chunks, shape):
    rows = chunks[0].shape[0]
    return pl.pallas_call(
        result_kernel,
        out_shape=jax.ShapeDtypeStruct(shape, bf16),
        in_specs=[SMEM_SPEC] * 2 + [VMEM_SPEC] * len(chunks),
        out_specs=VMEM_SPEC,
        compiler_params=pltpu.CompilerParams(vmem_limit_bytes=vmem_limit(rows)),
        name="result_rows",
    )(info, lengths, *map(in_vmem, chunks))


def body(tokens, lengths, norm_gain, gate_tiles, up_tiles, in_index, down_tiles, out_index):
    micro_count, own_count, model_width = tokens.shape
    block = gate_tiles.shape[-1]
    section_id = lax.axis_index("section")
    section_total = lax.axis_size("section")
    shard_total = lax.axis_size("shard")
    rows = live_total(tokens.shape, shard_total)
    info = jnp.stack([lax.axis_index("shard"), section_id])
    gain = norm_gain.reshape(model_width // block, block)
    held = in_vmem(load_weights(info, gate_tiles[0], up_tiles[0], rows))
    own_tokens = tokens.reshape(micro_count * own_count, model_width)
    came = same_core(own_tokens)[1:]
    chunks = both_cores([own_tokens, *relay(held, came, rows)])
    for turn in range(section_total):
        first = turn == 0
        parts = layer_step(
            first, rows, info, lengths, in_index[0], out_index[0], gain, held, down_tiles[0], chunks, micro_count, own_count
        )
        if first:
            x_own, kept, held = parts[2], parts[2], in_vmem(parts[3])
        else:
            x_own = chunks[0]
        sums = pair_sum(held, parts[0], xor_shard(parts[1], 1))
        came = [xor_shard(part, 2 * i + 2) for i, part in enumerate(sums[1:])]
        fresh, kept = finish_sum(turn, info, held, x_own, sums[0], came, kept)
        if turn + 1 < section_total:
            chunks = both_cores(next_section(fresh, turn))
    return result_rows(info, lengths, both_cores(same_core(kept)), tokens.shape)[None]


def solution(mesh):
    placed = (
        P(None, "shard", None),
        P(),
        P("section", None),
        P("section", "shard", None, None, None),
        P("section", "shard", None, None, None),
        P("section", "shard", None),
        P("section", "shard", None, None, None),
        P("section", "shard", None),
    )
    return jax.shard_map(
        body,
        mesh=mesh,
        in_specs=placed,
        out_specs=P("section", None, "shard", None),
        check_vma=False,
    )
```

```python
import functools

import jax
import jax.numpy as jnp
from jax import lax
from jax.experimental import pallas as pl
from jax.experimental.pallas import tpu as pltpu
from jax.sharding import PartitionSpec as P

norm_eps = 1e-05
f32 = jnp.float32
bf16 = jnp.bfloat16
MIB = 2**20
VMEM_SPEC = pl.BlockSpec(memory_space=pltpu.VMEM)
SMEM_SPEC = pl.BlockSpec(memory_space=pltpu.SMEM)
ANY_SPEC = pl.BlockSpec(memory_space=pl.ANY)


def live_total(tokens_shape, shard_total):
    micro_count, own_count, _ = tokens_shape
    return micro_count * own_count * shard_total * 5 // 8


def xor_shard(value, mask):
    size = lax.axis_size("shard")
    return lax.ppermute(value, "shard", [(i, i ^ mask) for i in range(size)])


def same_core(value):
    size = lax.axis_size("shard")
    return [value] + [xor_shard(value, mask) for mask in range(2, size, 2)]


def next_section(value, turn):
    size = lax.axis_size("shard")
    start = turn * size
    return [
        lax.ppermute(
            value,
            ("section", "shard"),
            [(start + i, start + size + (i ^ mask)) for i in range(size)],
        )
        for mask in range(0, size, 2)
    ]


def both_cores(parts):
    other_core = [xor_shard(part, 1) for part in parts]
    return [part for pair in zip(parts, other_core) for part in pair]


def vmem_limit(rows):
    return (12 if rows <= 64 else 32) * MIB


def in_vmem(value):
    return pltpu.with_memory_space_constraint(value, pltpu.VMEM)


def preloaded(blocks):
    return blocks // 2


def load_kernel(gate_ref, up_ref, held_ref, sems):
    early = preloaded(gate_ref.shape[0])

    def copies(h):
        return [
            pltpu.make_async_copy(ref.at[h], held_ref.at[i, h], sems.at[i, h])
            for i, ref in enumerate((gate_ref, up_ref))
        ]

    @pl.loop(0, early)
    def _(h):
        for copy in copies(h):
            copy.start()

    @pl.loop(0, early)
    def _(h):
        for copy in copies(h):
            copy.wait()


def load_weights(gate, up, rows):
    early = preloaded(gate.shape[0])
    return pl.pallas_call(
        load_kernel,
        out_shape=pltpu.VMEM((3,) + gate.shape, bf16),
        in_specs=[ANY_SPEC] * 2,
        out_specs=VMEM_SPEC,
        scratch_shapes=[pltpu.SemaphoreType.DMA((2, early))],
        compiler_params=pltpu.CompilerParams(vmem_limit_bytes=vmem_limit(rows)),
        cost_estimate=pl.CostEstimate(
            flops=0,
            bytes_accessed=4 * gate.size,
            transcendentals=0,
        ),
        name="load_weights",
    )(gate, up)


def relay_kernel(held_ref, *refs):
    half = len(refs) // 2
    for source, target in zip(refs[:half], refs[half:]):
        target[...] = source[...]


def relay(held, parts, rows):
    return pl.pallas_call(
        relay_kernel,
        out_shape=[pltpu.VMEM(part.shape, part.dtype) for part in parts],
        in_specs=[VMEM_SPEC] * (1 + len(parts)),
        out_specs=[VMEM_SPEC] * len(parts),
        compiler_params=pltpu.CompilerParams(vmem_limit_bytes=vmem_limit(rows)),
        name="relay",
    )(held, *map(in_vmem, parts))


def row_starts(lengths_ref, micro_count):
    starts = [jnp.int32(0)]
    for m in range(micro_count):
        starts.append(starts[-1] + lengths_ref[m])
    return starts


def own_rows(device, lengths_ref, rows, micro_count, own_count):
    starts = row_starts(lengths_ref, micro_count)
    group = micro_count * own_count
    place = lax.broadcasted_iota(jnp.int32, (group, rows), 1)
    local = lax.broadcasted_iota(jnp.int32, (group, rows), 0)
    target = jnp.full((group, rows), -1, jnp.int32)
    for m in range(micro_count):
        for q in range(own_count):
            row = device * own_count + q
            to = jnp.where(row < lengths_ref[m], starts[m] + row, -1)
            target = jnp.where(local == m * own_count + q, to, target)
    return (target == place).astype(f32)


def layer_kernel(turn, last, rows, unroll, shard_total, micro_count, own_count, *refs):
    first = turn == 0
    lengths_ref, in_ref, out_ref, gain_ref, held_ref = refs[:5]
    rest = list(refs[5:])
    sources = [rest.pop(0) for _ in range(3)] if first else None
    shard_id = lax.axis_index("shard")
    active = lax.axis_index("section") == turn
    blocks, slots, block = held_ref.shape[1], held_ref.shape[2], held_ref.shape[4]
    block_total = gain_ref.shape[0]
    chunk_blocks = block_total // shard_total
    chunks = [rest.pop(0) for _ in range(shard_total)]
    back_in_ref = None if first else rest.pop(0)
    even_ref, odd_ref = rest.pop(0), rest.pop(0)
    back_ref = None if first else rest.pop(0)
    if first:
        own_ref, filled_ref = rest.pop(0), rest.pop(0)
        sems = rest.pop()

        early = preloaded(blocks)

        def copy_in(i, h):
            return pltpu.make_async_copy(sources[i].at[h], filled_ref.at[i, h], sems.at[i, h])

        @pl.loop(early, blocks)
        def _(h):
            copy_in(0, h).start()
            copy_in(1, h).start()

        @pl.loop(0, blocks)
        def _(h):
            copy_in(2, h).start()
    else:
        filled_ref = held_ref
    normed, hidden, total = rest

    @pl.when(active)
    def _():
        squares = jnp.zeros((rows, block), f32)
        if first:
            starts = row_starts(lengths_ref, micro_count)
            group = micro_count * own_count
            place = lax.broadcasted_iota(jnp.int32, (rows, group), 0)
            local = lax.broadcasted_iota(jnp.int32, (rows, group), 1)
            picks = []
            for j in range(shard_total):
                device = shard_id ^ j
                target = jnp.full((rows, group), -1, jnp.int32)
                for m in range(micro_count):
                    for q in range(own_count):
                        row = device * own_count + q
                        to = jnp.where(row < lengths_ref[m], starts[m] + row, -1)
                        target = jnp.where(local == m * own_count + q, to, target)
                picks.append((target == place).astype(f32))
            pick = jnp.concatenate(picks, axis=1).astype(bf16)
            for c in range(shard_total):
                columns = pl.ds(c * chunk_blocks * block, chunk_blocks * block)
                spans = jnp.concatenate([ref[:, columns].astype(f32) for ref in chunks], axis=0)
                raw = jnp.dot(pick, spans.astype(bf16), preferred_element_type=f32)
                for i in range(chunk_blocks):
                    piece = raw[:, i * block : (i + 1) * block]
                    squares += piece * piece
                    normed[c * chunk_blocks + i] = piece.astype(bf16)
            for i in range(chunk_blocks):
                own_ref[:, i * block : (i + 1) * block] = normed[shard_id * chunk_blocks + i]
        else:
            for j in range(shard_total):
                base = (shard_id ^ j) * chunk_blocks
                for i in range(chunk_blocks):
                    piece = chunks[j][:, i * block : (i + 1) * block]
                    normed[base + i] = piece
                    wide = piece.astype(f32)
                    squares += wide * wide
        mean = jnp.sum(squares, axis=1, keepdims=True) / (block_total * block)
        scale = lax.rsqrt(mean + norm_eps)
        for b in range(block_total):
            normed[b] = (normed[b].astype(f32) * scale * gain_ref[b : b + 1, :]).astype(bf16)
        normed[block_total] = jnp.zeros((rows, block), bf16)
        total[...] = jnp.zeros_like(total)

        def at(ref, h, k):
            index = ref[h, k]
            return jnp.where(index < 0, block_total, index)

        @pl.loop(0, blocks // unroll)
        def _(step):
            if first:

                @pl.when(step * unroll >= early)
                def _():
                    for q in range(unroll):
                        copy_in(0, step * unroll + q).wait()
                        copy_in(1, step * unroll + q).wait()

            for q in range(unroll):
                h = step * unroll + q
                picked = jnp.concatenate([normed[at(in_ref, h, k)] for k in range(slots)], axis=1)
                gate = jnp.dot(
                    picked, filled_ref[0, h].reshape(slots * block, block), preferred_element_type=f32
                )
                up = jnp.dot(
                    picked, filled_ref[1, h].reshape(slots * block, block), preferred_element_type=f32
                )
                hidden[h] = (gate / (1.0 + jnp.exp(-gate)) * up).astype(bf16)

        @pl.loop(0, blocks // unroll)
        def _(step):
            if first:
                for q in range(unroll):
                    copy_in(2, step * unroll + q).wait()
            for q in range(unroll):
                h = step * unroll + q
                rows_in = hidden[h]
                for k in range(0, slots, 2):
                    pair = jnp.concatenate([filled_ref[2, h, k], filled_ref[2, h, k + 1]], axis=1)
                    product = jnp.dot(rows_in, pair, preferred_element_type=f32)
                    for p in range(2):
                        total[at(out_ref, h, k + p)] += product[:, p * block : (p + 1) * block]

        if not first:
            pick = own_rows(shard_id, lengths_ref, rows, micro_count, own_count).astype(bf16)
            for j in range(shard_total):
                width = chunk_blocks * block
                columns = pl.ds(pl.multiple_of((shard_id ^ j) * width, width), width)
                value = jnp.dot(pick, chunks[j][...], preferred_element_type=f32)
                back_ref[:, columns] = value.astype(bf16)
        if last:
            group = micro_count * own_count
            picks = [
                own_rows(shard_id ^ j, lengths_ref, rows, micro_count, own_count)
                for j in (*range(0, shard_total, 2), *range(1, shard_total, 2))
            ]
            pick = jnp.concatenate(picks, axis=0).astype(bf16)
            span = chunk_blocks
            for b in range(0, block_total, span):
                part = jnp.concatenate([total[b + i].astype(bf16) for i in range(span)], axis=1)
                value = jnp.dot(pick, part, preferred_element_type=f32)
                columns = slice(b * block, (b + span) * block)
                for j in range(shard_total):
                    target = even_ref if j < shard_total // 2 else odd_ref
                    piece = value[j * group : (j + 1) * group]
                    target[j % (shard_total // 2), :, columns] = piece.astype(bf16)
        else:
            for j in range(shard_total):
                base = (shard_id ^ j) * chunk_blocks
                target = (odd_ref if j % 2 else even_ref).at[j // 2]
                for i in range(chunk_blocks):
                    target[:, i * block : (i + 1) * block] = total[base + i].astype(bf16)

    if not first:

        @pl.when(jnp.logical_not(active))
        def _():
            back_ref[...] = back_in_ref[...]

    if first:

        @pl.when(jnp.logical_not(active))
        def _():
            @pl.loop(early, blocks)
            def _(h):
                copy_in(0, h).wait()
                copy_in(1, h).wait()

            @pl.loop(0, blocks)
            def _(h):
                copy_in(2, h).wait()


def layer_step(turn, last, rows, lengths, in_index, out_index, gain, held, tiles, chunks, back, micro_count, own_count):
    first = turn == 0
    shard_total = len(chunks)
    _, blocks, slots, block, _ = held.shape
    block_total = gain.shape[0]
    width = block_total * block // shard_total
    unroll = max(u for u in (1, 2, 4) if blocks % u == 0 and preloaded(blocks) % u == 0)
    group = micro_count * own_count
    part = (group, block_total * block) if last else (rows, width)
    outs = [pltpu.VMEM((shard_total // 2,) + part, bf16)] * 2
    if not first:
        outs.append(pltpu.VMEM(back.shape, bf16))
    if first:
        outs.append(pltpu.VMEM((rows, width), bf16))
        outs.append(pltpu.VMEM(held.shape, bf16))
    return pl.pallas_call(
        functools.partial(layer_kernel, turn, last, rows, unroll, shard_total, micro_count, own_count),
        out_shape=outs,
        in_specs=[SMEM_SPEC] * 3
        + [VMEM_SPEC] * 2
        + [ANY_SPEC] * (3 * first)
        + [VMEM_SPEC] * (shard_total + (not first)),
        out_specs=[VMEM_SPEC] * len(outs),
        scratch_shapes=[
            pltpu.VMEM((block_total + 1, rows, block), bf16),
            pltpu.VMEM((blocks, rows, block), bf16),
            pltpu.VMEM((block_total + 1, rows, block), f32),
        ]
        + ([pltpu.SemaphoreType.DMA((3, blocks))] if first else []),
        compiler_params=pltpu.CompilerParams(vmem_limit_bytes=vmem_limit(rows)),
        cost_estimate=pl.CostEstimate(
            flops=2 * rows * held.size, bytes_accessed=0, transcendentals=0
        ),
        input_output_aliases={4: 3} if first else {},
        name=f"layer_{turn}",
    )(lengths, in_index, out_index, gain, held, *(tiles if first else ()), *map(in_vmem, chunks), *(() if first else (in_vmem(back),)))


def pair_kernel(held_ref, even_ref, came_ref, own_ref, *send_refs):
    own_ref[...] = even_ref[0].astype(f32) + came_ref[0].astype(f32)
    for i, ref in enumerate(send_refs):
        ref[...] = (even_ref[i + 1].astype(f32) + came_ref[i + 1].astype(f32)).astype(bf16)


def pair_sum(held, even, came):
    parts, rows, width = even.shape
    return pl.pallas_call(
        pair_kernel,
        out_shape=[pltpu.VMEM((rows, width), f32)] + [pltpu.VMEM((rows, width), bf16)] * (parts - 1),
        in_specs=[VMEM_SPEC] * 3,
        out_specs=[VMEM_SPEC] * parts,
        compiler_params=pltpu.CompilerParams(vmem_limit_bytes=vmem_limit(rows)),
        name="pair_sum",
    )(held, in_vmem(even), in_vmem(came))


def finish_kernel(held_ref, x_ref, own_ref, *refs):
    sum_value = own_ref[...]
    for ref in refs[:-1]:
        sum_value = sum_value + ref[...].astype(f32)
    refs[-1][...] = (x_ref[...].astype(f32) + sum_value).astype(bf16)


def finish_sum(held, x_own, own, came):
    rows, width = x_own.shape
    return pl.pallas_call(
        finish_kernel,
        out_shape=pltpu.VMEM((rows, width), bf16),
        in_specs=[VMEM_SPEC] * (3 + len(came)),
        out_specs=VMEM_SPEC,
        compiler_params=pltpu.CompilerParams(vmem_limit_bytes=vmem_limit(rows)),
        name="finish_sum",
    )(held, *map(in_vmem, (x_own, own, *came)))


def result_kernel(last_turn, later_ref, x_ref, own_ref, *refs):
    out_ref = refs[-1]
    micro_count, own_count, _ = out_ref.shape
    sum_value = own_ref[...]
    for ref in refs[:-1]:
        sum_value = sum_value + ref[...].astype(f32)
    fresh = x_ref[...].astype(f32) + sum_value
    mine = lax.axis_index("section") == last_turn
    value = jnp.where(mine, fresh, later_ref[...].astype(f32))
    for m in range(micro_count):
        out_ref[m] = value[m * own_count : (m + 1) * own_count].astype(bf16)


def result_rows(last_turn, later, x_own, own, came, shape):
    return pl.pallas_call(
        functools.partial(result_kernel, last_turn),
        out_shape=jax.ShapeDtypeStruct(shape, bf16),
        in_specs=[VMEM_SPEC] * (3 + len(came)),
        out_specs=VMEM_SPEC,
        compiler_params=pltpu.CompilerParams(vmem_limit_bytes=vmem_limit(x_own.shape[0])),
        name="result_rows",
    )(*map(in_vmem, (later, x_own, own, *came)))


def body(tokens, lengths, norm_gain, gate_tiles, up_tiles, in_index, down_tiles, out_index):
    micro_count, own_count, model_width = tokens.shape
    block = gate_tiles.shape[-1]
    section_total = lax.axis_size("section")
    shard_total = lax.axis_size("shard")
    rows = live_total(tokens.shape, shard_total)
    gain = in_vmem(norm_gain.reshape(model_width // block, block))
    in_index, out_index, lengths = [
        pltpu.with_memory_space_constraint(value, pltpu.SMEM) for value in (in_index[0], out_index[0], lengths)
    ]
    tiles = (gate_tiles[0], up_tiles[0], down_tiles[0])
    held = in_vmem(load_weights(*tiles[:2], rows))
    own_tokens = tokens.reshape(micro_count * own_count, model_width)
    came = same_core(own_tokens)[1:]
    chunks = both_cores([own_tokens, *relay(held, came, rows)])
    back = own_tokens
    for turn in range(section_total):
        first, last = turn == 0, turn + 1 == section_total
        parts = layer_step(
            turn, last, rows, lengths, in_index, out_index, gain, held, tiles, chunks, back, micro_count, own_count
        )
        if first:
            x_own, held = parts[2], in_vmem(parts[3])
        else:
            x_own, back = chunks[0], parts[2]
        sums = pair_sum(held, parts[0], xor_shard(parts[1], 1))
        came = [xor_shard(part, 2 * i + 2) for i, part in enumerate(sums[1:])]
        if not last:
            fresh = finish_sum(held, x_own, sums[0], came)
            chunks = both_cores(next_section(fresh, turn))
    later = lax.ppermute(back, "section", [(i + 1, i) for i in range(section_total - 1)])
    return result_rows(section_total - 1, later, back, sums[0], came, tokens.shape)[None]


def solution(mesh):
    placed = (
        P(None, "shard", None),
        P(),
        P("section", None),
        P("section", "shard", None, None, None),
        P("section", "shard", None, None, None),
        P("section", "shard", None),
        P("section", "shard", None, None, None),
        P("section", "shard", None),
    )
    return jax.shard_map(
        body,
        mesh=mesh,
        in_specs=placed,
        out_specs=P("section", None, "shard", None),
        check_vma=False,
    )
```

```python
import functools

import jax
import jax.numpy as jnp
from jax import lax
from jax.experimental import pallas as pl
from jax.experimental.pallas import tpu as pltpu
from jax.sharding import PartitionSpec as P

norm_eps = 1e-05
f32 = jnp.float32
bf16 = jnp.bfloat16
MIB = 2**20
VMEM_SPEC = pl.BlockSpec(memory_space=pltpu.VMEM)
ANY_SPEC = pl.BlockSpec(memory_space=pl.ANY)


def live_total(tokens_shape, shard_total):
    micro_count, own_count, _ = tokens_shape
    return micro_count * own_count * shard_total * 5 // 8


def xor_shard(value, mask):
    size = lax.axis_size("shard")
    return lax.ppermute(value, "shard", [(i, i ^ mask) for i in range(size)])


def same_core(value):
    size = lax.axis_size("shard")
    return [value] + [xor_shard(value, mask) for mask in range(2, size, 2)]


def next_section(value, turn):
    size = lax.axis_size("shard")
    start = turn * size
    return [
        lax.ppermute(
            value,
            ("section", "shard"),
            [(start + i, start + size + (i ^ mask)) for i in range(size)],
        )
        for mask in range(0, size, 2)
    ]


def both_cores(parts):
    other_core = [xor_shard(part, 1) for part in parts]
    return [part for pair in zip(parts, other_core) for part in pair]


def vmem_limit(rows):
    return (12 if rows <= 64 else 32) * MIB


def in_vmem(value):
    return pltpu.with_memory_space_constraint(value, pltpu.VMEM)


def preloaded(blocks):
    return blocks // 2


def load_kernel(gate_ref, up_ref, held_ref, sems):
    early = preloaded(gate_ref.shape[0])

    def copies(h):
        return [
            pltpu.make_async_copy(ref.at[h], held_ref.at[i, h], sems.at[i, h])
            for i, ref in enumerate((gate_ref, up_ref))
        ]

    @pl.loop(0, early)
    def _(h):
        for copy in copies(h):
            copy.start()

    @pl.loop(0, early)
    def _(h):
        for copy in copies(h):
            copy.wait()


def load_weights(gate, up, rows):
    early = preloaded(gate.shape[0])
    return pl.pallas_call(
        load_kernel,
        out_shape=pltpu.VMEM((3,) + gate.shape, bf16),
        in_specs=[ANY_SPEC] * 2,
        out_specs=VMEM_SPEC,
        scratch_shapes=[pltpu.SemaphoreType.DMA((2, early))],
        compiler_params=pltpu.CompilerParams(vmem_limit_bytes=vmem_limit(rows)),
        cost_estimate=pl.CostEstimate(
            flops=0,
            bytes_accessed=4 * gate.size,
            transcendentals=0,
        ),
        name="load_weights",
    )(gate, up)


def relay_kernel(held_ref, *refs):
    half = len(refs) // 2
    for source, target in zip(refs[:half], refs[half:]):
        target[...] = source[...]


def relay(held, parts, rows):
    return pl.pallas_call(
        relay_kernel,
        out_shape=[pltpu.VMEM(part.shape, part.dtype) for part in parts],
        in_specs=[VMEM_SPEC] * (1 + len(parts)),
        out_specs=[VMEM_SPEC] * len(parts),
        compiler_params=pltpu.CompilerParams(vmem_limit_bytes=vmem_limit(rows)),
        name="relay",
    )(held, *map(in_vmem, parts))


def row_starts(lengths_ref, micro_count):
    starts = [jnp.int32(0)]
    for m in range(micro_count):
        starts.append(starts[-1] + lengths_ref[m])
    return starts


def own_rows(device, lengths_ref, rows, micro_count, own_count):
    starts = row_starts(lengths_ref, micro_count)
    group = micro_count * own_count
    place = lax.broadcasted_iota(jnp.int32, (group, rows), 1)
    local = lax.broadcasted_iota(jnp.int32, (group, rows), 0)
    target = jnp.full((group, rows), -1, jnp.int32)
    for m in range(micro_count):
        for q in range(own_count):
            row = device * own_count + q
            to = jnp.where(row < lengths_ref[m], starts[m] + row, -1)
            target = jnp.where(local == m * own_count + q, to, target)
    return (target == place).astype(f32)


def layer_kernel(turn, last, rows, unroll, shard_total, micro_count, own_count, *refs):
    first = turn == 0
    scalars, (gain_ref, held_ref) = refs[:3], refs[3:5]
    rest = list(refs[5:])
    sources = [rest.pop(0) for _ in range(3)] if first else None
    shard_id = lax.axis_index("shard")
    active = lax.axis_index("section") == turn
    blocks, slots, block = held_ref.shape[1], held_ref.shape[2], held_ref.shape[4]
    block_total = gain_ref.shape[0]
    chunk_blocks = block_total // shard_total
    chunks = [rest.pop(0) for _ in range(shard_total)]
    back_in_ref = None if first else rest.pop(0)
    even_ref, odd_ref = rest.pop(0), rest.pop(0)
    back_ref = None if first else rest.pop(0)
    own_ref, filled_ref = (rest.pop(0), rest.pop(0)) if first else (None, held_ref)
    sems = rest.pop() if first else None
    normed, hidden, total, lengths_ref, in_ref, out_ref, scalar_sems = rest
    places = (lengths_ref, in_ref, out_ref)
    lengths_copy, in_copy, out_copy = [
        pltpu.make_async_copy(scalars[i], places[i], scalar_sems.at[i]) for i in range(3)
    ]
    for copy in (lengths_copy, in_copy, out_copy):
        copy.start()
    if first:
        early = preloaded(blocks)

        def copy_in(i, h):
            return pltpu.make_async_copy(sources[i].at[h], filled_ref.at[i, h], sems.at[i, h])

        @pl.loop(early, blocks)
        def _(h):
            copy_in(0, h).start()
            copy_in(1, h).start()

        @pl.loop(0, blocks)
        def _(h):
            copy_in(2, h).start()

    @pl.when(active)
    def _():
        squares = jnp.zeros((rows, block), f32)
        if first:
            lengths_copy.wait()
            starts = row_starts(lengths_ref, micro_count)
            group = micro_count * own_count
            place = lax.broadcasted_iota(jnp.int32, (rows, group), 0)
            local = lax.broadcasted_iota(jnp.int32, (rows, group), 1)
            picks = []
            for j in range(shard_total):
                device = shard_id ^ j
                target = jnp.full((rows, group), -1, jnp.int32)
                for m in range(micro_count):
                    for q in range(own_count):
                        row = device * own_count + q
                        to = jnp.where(row < lengths_ref[m], starts[m] + row, -1)
                        target = jnp.where(local == m * own_count + q, to, target)
                picks.append((target == place).astype(f32))
            pick = jnp.concatenate(picks, axis=1).astype(bf16)
            for c in range(shard_total):
                columns = pl.ds(c * chunk_blocks * block, chunk_blocks * block)
                spans = jnp.concatenate([ref[:, columns].astype(f32) for ref in chunks], axis=0)
                raw = jnp.dot(pick, spans.astype(bf16), preferred_element_type=f32)
                for i in range(chunk_blocks):
                    piece = raw[:, i * block : (i + 1) * block]
                    squares += piece * piece
                    normed[c * chunk_blocks + i] = piece.astype(bf16)
            for i in range(chunk_blocks):
                own_ref[:, i * block : (i + 1) * block] = normed[shard_id * chunk_blocks + i]
        else:
            for j in range(shard_total):
                base = (shard_id ^ j) * chunk_blocks
                for i in range(chunk_blocks):
                    piece = chunks[j][:, i * block : (i + 1) * block]
                    normed[base + i] = piece
                    wide = piece.astype(f32)
                    squares += wide * wide
        mean = jnp.sum(squares, axis=1, keepdims=True) / (block_total * block)
        scale = lax.rsqrt(mean + norm_eps)
        for b in range(block_total):
            normed[b] = (normed[b].astype(f32) * scale * gain_ref[b : b + 1, :]).astype(bf16)
        normed[block_total] = jnp.zeros((rows, block), bf16)
        total[...] = jnp.zeros_like(total)

        def at(ref, h, k):
            index = ref[h, k]
            return jnp.where(index < 0, block_total, index)

        in_copy.wait()

        @pl.loop(0, blocks // unroll)
        def _(step):
            if first:

                @pl.when(step * unroll >= early)
                def _():
                    for q in range(unroll):
                        copy_in(0, step * unroll + q).wait()
                        copy_in(1, step * unroll + q).wait()

            for q in range(unroll):
                h = step * unroll + q
                picked = jnp.concatenate([normed[at(in_ref, h, k)] for k in range(slots)], axis=1)
                gate = jnp.dot(
                    picked, filled_ref[0, h].reshape(slots * block, block), preferred_element_type=f32
                )
                up = jnp.dot(
                    picked, filled_ref[1, h].reshape(slots * block, block), preferred_element_type=f32
                )
                hidden[h] = (gate / (1.0 + jnp.exp(-gate)) * up).astype(bf16)

        out_copy.wait()

        @pl.loop(0, blocks // unroll)
        def _(step):
            if first:
                for q in range(unroll):
                    copy_in(2, step * unroll + q).wait()
            for q in range(unroll):
                h = step * unroll + q
                rows_in = hidden[h]
                for k in range(0, slots, 2):
                    pair = jnp.concatenate([filled_ref[2, h, k], filled_ref[2, h, k + 1]], axis=1)
                    product = jnp.dot(rows_in, pair, preferred_element_type=f32)
                    for p in range(2):
                        total[at(out_ref, h, k + p)] += product[:, p * block : (p + 1) * block]

        if not first:
            lengths_copy.wait()
            pick = own_rows(shard_id, lengths_ref, rows, micro_count, own_count).astype(bf16)
            for j in range(shard_total):
                width = chunk_blocks * block
                columns = pl.ds(pl.multiple_of((shard_id ^ j) * width, width), width)
                value = jnp.dot(pick, chunks[j][...], preferred_element_type=f32)
                back_ref[:, columns] = value.astype(bf16)
        if last:
            group = micro_count * own_count
            picks = [
                own_rows(shard_id ^ j, lengths_ref, rows, micro_count, own_count)
                for j in (*range(0, shard_total, 2), *range(1, shard_total, 2))
            ]
            pick = jnp.concatenate(picks, axis=0).astype(bf16)
            span = chunk_blocks
            for b in range(0, block_total, span):
                part = jnp.concatenate([total[b + i].astype(bf16) for i in range(span)], axis=1)
                value = jnp.dot(pick, part, preferred_element_type=f32)
                columns = slice(b * block, (b + span) * block)
                for j in range(shard_total):
                    target = even_ref if j < shard_total // 2 else odd_ref
                    piece = value[j * group : (j + 1) * group]
                    target[j % (shard_total // 2), :, columns] = piece.astype(bf16)
        else:
            for j in range(shard_total):
                base = (shard_id ^ j) * chunk_blocks
                target = (odd_ref if j % 2 else even_ref).at[j // 2]
                for i in range(chunk_blocks):
                    target[:, i * block : (i + 1) * block] = total[base + i].astype(bf16)

    @pl.when(jnp.logical_not(active))
    def _():
        for copy in (lengths_copy, in_copy, out_copy):
            copy.wait()
        if first:

            @pl.loop(early, blocks)
            def _(h):
                copy_in(0, h).wait()
                copy_in(1, h).wait()

            @pl.loop(0, blocks)
            def _(h):
                copy_in(2, h).wait()

        else:
            back_ref[...] = back_in_ref[...]


def layer_step(turn, last, rows, lengths, in_index, out_index, gain, held, tiles, chunks, back, micro_count, own_count):
    first = turn == 0
    shard_total = len(chunks)
    _, blocks, slots, block, _ = held.shape
    block_total = gain.shape[0]
    width = block_total * block // shard_total
    whole = preloaded(blocks) if first else blocks
    unroll = max(u for u in ((1, 2, 4) if first else (1, 2, 4, 8)) if blocks % u == 0 and whole % u == 0)
    group = micro_count * own_count
    part = (group, block_total * block) if last else (rows, width)
    outs = [pltpu.VMEM((shard_total // 2,) + part, bf16)] * 2
    if not first:
        outs.append(pltpu.VMEM(back.shape, bf16))
    if first:
        outs.append(pltpu.VMEM((rows, width), bf16))
        outs.append(pltpu.VMEM(held.shape, bf16))
    return pl.pallas_call(
        functools.partial(layer_kernel, turn, last, rows, unroll, shard_total, micro_count, own_count),
        out_shape=outs,
        in_specs=[ANY_SPEC] * 3
        + [VMEM_SPEC] * 2
        + [ANY_SPEC] * (3 * first)
        + [VMEM_SPEC] * (shard_total + (not first)),
        out_specs=[VMEM_SPEC] * len(outs),
        scratch_shapes=[
            pltpu.VMEM((block_total + 1, rows, block), bf16),
            pltpu.VMEM((blocks, rows, block), bf16),
            pltpu.VMEM((block_total + 1, rows, block), f32),
            pltpu.SMEM(lengths.shape, jnp.int32),
            pltpu.SMEM(in_index.shape, jnp.int32),
            pltpu.SMEM(out_index.shape, jnp.int32),
            pltpu.SemaphoreType.DMA((3,)),
        ]
        + ([pltpu.SemaphoreType.DMA((3, blocks))] if first else []),
        compiler_params=pltpu.CompilerParams(vmem_limit_bytes=vmem_limit(rows)),
        cost_estimate=pl.CostEstimate(
            flops=2 * rows * held.size, bytes_accessed=0, transcendentals=0
        ),
        input_output_aliases={4: 3} if first else {},
        name=f"layer_{turn}",
    )(lengths, in_index, out_index, gain, held, *(tiles if first else ()), *map(in_vmem, chunks), *(() if first else (in_vmem(back),)))


def pair_kernel(held_ref, even_ref, came_ref, own_ref, *send_refs):
    own_ref[...] = even_ref[0].astype(f32) + came_ref[0].astype(f32)
    for i, ref in enumerate(send_refs):
        ref[...] = (even_ref[i + 1].astype(f32) + came_ref[i + 1].astype(f32)).astype(bf16)


def pair_sum(held, even, came):
    parts, rows, width = even.shape
    return pl.pallas_call(
        pair_kernel,
        out_shape=[pltpu.VMEM((rows, width), f32)] + [pltpu.VMEM((rows, width), bf16)] * (parts - 1),
        in_specs=[VMEM_SPEC] * 3,
        out_specs=[VMEM_SPEC] * parts,
        compiler_params=pltpu.CompilerParams(vmem_limit_bytes=vmem_limit(rows)),
        name="pair_sum",
    )(held, in_vmem(even), in_vmem(came))


def finish_kernel(held_ref, x_ref, own_ref, *refs):
    sum_value = own_ref[...]
    for ref in refs[:-1]:
        sum_value = sum_value + ref[...].astype(f32)
    refs[-1][...] = (x_ref[...].astype(f32) + sum_value).astype(bf16)


def finish_sum(held, x_own, own, came):
    rows, width = x_own.shape
    return pl.pallas_call(
        finish_kernel,
        out_shape=pltpu.VMEM((rows, width), bf16),
        in_specs=[VMEM_SPEC] * (3 + len(came)),
        out_specs=VMEM_SPEC,
        compiler_params=pltpu.CompilerParams(vmem_limit_bytes=vmem_limit(rows)),
        name="finish_sum",
    )(held, *map(in_vmem, (x_own, own, *came)))


def result_kernel(last_turn, later_ref, x_ref, own_ref, *refs):
    out_ref = refs[-1]
    micro_count, own_count, _ = out_ref.shape
    sum_value = own_ref[...]
    for ref in refs[:-1]:
        sum_value = sum_value + ref[...].astype(f32)
    fresh = x_ref[...].astype(f32) + sum_value
    mine = lax.axis_index("section") == last_turn
    value = jnp.where(mine, fresh, later_ref[...].astype(f32))
    for m in range(micro_count):
        out_ref[m] = value[m * own_count : (m + 1) * own_count].astype(bf16)


def result_rows(last_turn, later, x_own, own, came, shape):
    return pl.pallas_call(
        functools.partial(result_kernel, last_turn),
        out_shape=jax.ShapeDtypeStruct(shape, bf16),
        in_specs=[VMEM_SPEC] * (3 + len(came)),
        out_specs=VMEM_SPEC,
        compiler_params=pltpu.CompilerParams(vmem_limit_bytes=vmem_limit(x_own.shape[0])),
        name="result_rows",
    )(*map(in_vmem, (later, x_own, own, *came)))


def body(tokens, lengths, norm_gain, gate_tiles, up_tiles, in_index, down_tiles, out_index):
    micro_count, own_count, model_width = tokens.shape
    block = gate_tiles.shape[-1]
    section_total = lax.axis_size("section")
    shard_total = lax.axis_size("shard")
    rows = live_total(tokens.shape, shard_total)
    gain = in_vmem(norm_gain.reshape(model_width // block, block))
    in_index, out_index = in_index[0], out_index[0]
    tiles = (gate_tiles[0], up_tiles[0], down_tiles[0])
    held = in_vmem(load_weights(*tiles[:2], rows))
    own_tokens = tokens.reshape(micro_count * own_count, model_width)
    came = same_core(own_tokens)[1:]
    chunks = both_cores([own_tokens, *relay(held, came, rows)])
    back = own_tokens
    for turn in range(section_total):
        first, last = turn == 0, turn + 1 == section_total
        parts = layer_step(
            turn, last, rows, lengths, in_index, out_index, gain, held, tiles, chunks, back, micro_count, own_count
        )
        if first:
            x_own, held = parts[2], in_vmem(parts[3])
        else:
            x_own, back = chunks[0], parts[2]
        sums = pair_sum(held, parts[0], xor_shard(parts[1], 1))
        came = [xor_shard(part, 2 * i + 2) for i, part in enumerate(sums[1:])]
        if not last:
            fresh = finish_sum(held, x_own, sums[0], came)
            chunks = both_cores(next_section(fresh, turn))
    later = lax.ppermute(back, "section", [(i + 1, i) for i in range(section_total - 1)])
    return result_rows(section_total - 1, later, back, sums[0], came, tokens.shape)[None]


def solution(mesh):
    placed = (
        P(None, "shard", None),
        P(),
        P("section", None),
        P("section", "shard", None, None, None),
        P("section", "shard", None, None, None),
        P("section", "shard", None),
        P("section", "shard", None, None, None),
        P("section", "shard", None),
    )
    return jax.shard_map(
        body,
        mesh=mesh,
        in_specs=placed,
        out_specs=P("section", None, "shard", None),
        check_vma=False,
    )
```

```python
import functools

import jax
import jax.numpy as jnp
from jax import lax
from jax.experimental import pallas as pl
from jax.experimental.pallas import tpu as pltpu
from jax.sharding import PartitionSpec as P

norm_eps = 1e-05
f32 = jnp.float32
bf16 = jnp.bfloat16
MIB = 2**20
VMEM_SPEC = pl.BlockSpec(memory_space=pltpu.VMEM)
ANY_SPEC = pl.BlockSpec(memory_space=pl.ANY)


def live_total(tokens_shape, shard_total):
    micro_count, own_count, _ = tokens_shape
    return micro_count * own_count * shard_total * 5 // 8


def xor_shard(value, mask):
    size = lax.axis_size("shard")
    return lax.ppermute(value, "shard", [(i, i ^ mask) for i in range(size)])


def same_core(value):
    size = lax.axis_size("shard")
    return [value] + [xor_shard(value, mask) for mask in range(2, size, 2)]


def next_section(value, turn):
    size = lax.axis_size("shard")
    start = turn * size
    return [
        lax.ppermute(
            value,
            ("section", "shard"),
            [(start + i, start + size + (i ^ mask)) for i in range(size)],
        )
        for mask in range(0, size, 2)
    ]


def both_cores(parts):
    other_core = [xor_shard(part, 1) for part in parts]
    return [part for pair in zip(parts, other_core) for part in pair]


def vmem_limit(rows):
    return (12 if rows <= 64 else 32) * MIB


def in_vmem(value):
    return pltpu.with_memory_space_constraint(value, pltpu.VMEM)


def preloaded(blocks):
    return blocks // 2


def load_kernel(gate_ref, up_ref, held_ref, sems):
    early = preloaded(gate_ref.shape[0])

    def copies(h):
        return [
            pltpu.make_async_copy(ref.at[h], held_ref.at[i, h], sems.at[i, h])
            for i, ref in enumerate((gate_ref, up_ref))
        ]

    @pl.loop(0, early)
    def _(h):
        for copy in copies(h):
            copy.start()

    @pl.loop(0, early)
    def _(h):
        for copy in copies(h):
            copy.wait()


def load_weights(gate, up, rows):
    early = preloaded(gate.shape[0])
    return pl.pallas_call(
        load_kernel,
        out_shape=pltpu.VMEM((3,) + gate.shape, bf16),
        in_specs=[ANY_SPEC] * 2,
        out_specs=VMEM_SPEC,
        scratch_shapes=[pltpu.SemaphoreType.DMA((2, early))],
        compiler_params=pltpu.CompilerParams(vmem_limit_bytes=vmem_limit(rows)),
        cost_estimate=pl.CostEstimate(
            flops=0,
            bytes_accessed=4 * gate.size,
            transcendentals=0,
        ),
        name="load_weights",
    )(gate, up)


def relay_kernel(held_ref, *refs):
    half = len(refs) // 2
    for source, target in zip(refs[:half], refs[half:]):
        target[...] = source[...]


def relay(held, parts, rows):
    return pl.pallas_call(
        relay_kernel,
        out_shape=[pltpu.VMEM(part.shape, part.dtype) for part in parts],
        in_specs=[VMEM_SPEC] * (1 + len(parts)),
        out_specs=[VMEM_SPEC] * len(parts),
        compiler_params=pltpu.CompilerParams(vmem_limit_bytes=vmem_limit(rows)),
        name="relay",
    )(held, *map(in_vmem, parts))


def row_starts(lengths_ref, micro_count):
    starts = [jnp.int32(0)]
    for m in range(micro_count):
        starts.append(starts[-1] + lengths_ref[m])
    return starts


def own_rows(device, lengths_ref, rows, micro_count, own_count):
    starts = row_starts(lengths_ref, micro_count)
    group = micro_count * own_count
    place = lax.broadcasted_iota(jnp.int32, (group, rows), 1)
    local = lax.broadcasted_iota(jnp.int32, (group, rows), 0)
    target = jnp.full((group, rows), -1, jnp.int32)
    for m in range(micro_count):
        for q in range(own_count):
            row = device * own_count + q
            to = jnp.where(row < lengths_ref[m], starts[m] + row, -1)
            target = jnp.where(local == m * own_count + q, to, target)
    return (target == place).astype(f32)


def layer_kernel(turn, last, rows, unroll, shard_total, micro_count, own_count, *refs):
    first = turn == 0
    scalars, (gain_ref, held_ref) = refs[:3], refs[3:5]
    rest = list(refs[5:])
    sources = [rest.pop(0) for _ in range(3)] if first else None
    shard_id = lax.axis_index("shard")
    active = lax.axis_index("section") == turn
    blocks, slots, block = held_ref.shape[1], held_ref.shape[2], held_ref.shape[4]
    block_total = gain_ref.shape[0]
    chunk_blocks = block_total // shard_total
    chunks = [rest.pop(0) for _ in range(shard_total)]
    back_in_ref = None if first else rest.pop(0)
    even_ref, odd_ref = rest.pop(0), rest.pop(0)
    back_ref = None if first else rest.pop(0)
    own_ref, filled_ref = (rest.pop(0), rest.pop(0)) if first else (None, held_ref)
    sems = rest.pop() if first else None
    normed, hidden, total, lengths_ref, in_ref, out_ref, scalar_sems = rest
    places = (lengths_ref, in_ref, out_ref)
    lengths_copy, in_copy, out_copy = [
        pltpu.make_async_copy(scalars[i], places[i], scalar_sems.at[i]) for i in range(3)
    ]
    for copy in (lengths_copy, in_copy, out_copy):
        copy.start()
    if first:
        early = preloaded(blocks)

        def copy_in(i, h):
            return pltpu.make_async_copy(sources[i].at[h], filled_ref.at[i, h], sems.at[i, h])

        @pl.loop(early, blocks)
        def _(h):
            copy_in(0, h).start()
            copy_in(1, h).start()

        @pl.loop(0, blocks)
        def _(h):
            copy_in(2, h).start()

    @pl.when(active)
    def _():
        squares = jnp.zeros((rows, block), f32)
        if first:
            lengths_copy.wait()
            starts = row_starts(lengths_ref, micro_count)
            group = micro_count * own_count
            place = lax.broadcasted_iota(jnp.int32, (rows, group), 0)
            local = lax.broadcasted_iota(jnp.int32, (rows, group), 1)
            picks = []
            for j in range(shard_total):
                device = shard_id ^ j
                target = jnp.full((rows, group), -1, jnp.int32)
                for m in range(micro_count):
                    for q in range(own_count):
                        row = device * own_count + q
                        to = jnp.where(row < lengths_ref[m], starts[m] + row, -1)
                        target = jnp.where(local == m * own_count + q, to, target)
                picks.append((target == place).astype(f32))
            pick = jnp.concatenate(picks, axis=1).astype(bf16)
            for c in range(shard_total):
                columns = pl.ds(c * chunk_blocks * block, chunk_blocks * block)
                spans = jnp.concatenate([ref[:, columns].astype(f32) for ref in chunks], axis=0)
                raw = jnp.dot(pick, spans.astype(bf16), preferred_element_type=f32)
                for i in range(chunk_blocks):
                    piece = raw[:, i * block : (i + 1) * block]
                    squares += piece * piece
                    normed[c * chunk_blocks + i] = piece.astype(bf16)
            for i in range(chunk_blocks):
                own_ref[:, i * block : (i + 1) * block] = normed[shard_id * chunk_blocks + i]
        else:
            for j in range(shard_total):
                base = (shard_id ^ j) * chunk_blocks
                for i in range(chunk_blocks):
                    piece = chunks[j][:, i * block : (i + 1) * block]
                    normed[base + i] = piece
                    wide = piece.astype(f32)
                    squares += wide * wide
        mean = jnp.sum(squares, axis=1, keepdims=True) / (block_total * block)
        scale = lax.rsqrt(mean + norm_eps)
        for b in range(block_total):
            normed[b] = (normed[b].astype(f32) * scale * gain_ref[b : b + 1, :]).astype(bf16)
        normed[block_total] = jnp.zeros((rows, block), bf16)
        total[...] = jnp.zeros_like(total)

        def at(ref, h, k):
            index = ref[h, k]
            return jnp.where(index < 0, block_total, index)

        in_copy.wait()

        @pl.loop(0, blocks // unroll)
        def _(step):
            if first:

                @pl.when(step * unroll >= early)
                def _():
                    for q in range(unroll):
                        copy_in(0, step * unroll + q).wait()
                        copy_in(1, step * unroll + q).wait()

            for q in range(unroll):
                h = step * unroll + q
                picked = jnp.concatenate([normed[at(in_ref, h, k)] for k in range(slots)], axis=1)
                gate = jnp.dot(
                    picked, filled_ref[0, h].reshape(slots * block, block), preferred_element_type=f32
                )
                up = jnp.dot(
                    picked, filled_ref[1, h].reshape(slots * block, block), preferred_element_type=f32
                )
                hidden[h] = (gate / (1.0 + jnp.exp(-gate)) * up).astype(bf16)

        out_copy.wait()

        @pl.loop(0, blocks // unroll)
        def _(step):
            if first:
                for q in range(unroll):
                    copy_in(2, step * unroll + q).wait()
            for q in range(unroll):
                h = step * unroll + q
                rows_in = hidden[h]
                for k in range(0, slots, 2):
                    pair = jnp.concatenate([filled_ref[2, h, k], filled_ref[2, h, k + 1]], axis=1)
                    product = jnp.dot(rows_in, pair, preferred_element_type=f32)
                    for p in range(2):
                        total[at(out_ref, h, k + p)] += product[:, p * block : (p + 1) * block]

        if not first:
            lengths_copy.wait()
            pick = own_rows(shard_id, lengths_ref, rows, micro_count, own_count).astype(bf16)
            for j in range(shard_total):
                width = chunk_blocks * block
                columns = pl.ds(pl.multiple_of((shard_id ^ j) * width, width), width)
                value = jnp.dot(pick, chunks[j][...], preferred_element_type=f32)
                back_ref[:, columns] = value.astype(bf16)
        if last:
            group = micro_count * own_count
            picks = [
                own_rows(shard_id ^ j, lengths_ref, rows, micro_count, own_count)
                for j in (*range(0, shard_total, 2), *range(1, shard_total, 2))
            ]
            pick = jnp.concatenate(picks, axis=0).astype(bf16)
            span = chunk_blocks
            for b in range(0, block_total, span):
                part = jnp.concatenate([total[b + i].astype(bf16) for i in range(span)], axis=1)
                value = jnp.dot(pick, part, preferred_element_type=f32)
                columns = slice(b * block, (b + span) * block)
                for j in range(shard_total):
                    target = even_ref if j < shard_total // 2 else odd_ref
                    piece = value[j * group : (j + 1) * group]
                    target[j % (shard_total // 2), :, columns] = piece.astype(bf16)
        else:
            for j in range(shard_total):
                base = (shard_id ^ j) * chunk_blocks
                target = (odd_ref if j % 2 else even_ref).at[j // 2]
                for i in range(chunk_blocks):
                    target[:, i * block : (i + 1) * block] = total[base + i].astype(bf16)

    @pl.when(jnp.logical_not(active))
    def _():
        for copy in (lengths_copy, in_copy, out_copy):
            copy.wait()
        if first:

            @pl.loop(early, blocks)
            def _(h):
                copy_in(0, h).wait()
                copy_in(1, h).wait()

            @pl.loop(0, blocks)
            def _(h):
                copy_in(2, h).wait()

        else:
            back_ref[...] = back_in_ref[...]


def layer_step(turn, last, rows, lengths, in_index, out_index, gain, held, tiles, chunks, back, micro_count, own_count):
    first = turn == 0
    shard_total = len(chunks)
    _, blocks, slots, block, _ = held.shape
    block_total = gain.shape[0]
    width = block_total * block // shard_total
    whole = preloaded(blocks) if first else blocks
    unroll = max(u for u in ((1, 2, 4) if first else (1, 2, 4, 8, 16)) if blocks % u == 0 and whole % u == 0)
    group = micro_count * own_count
    part = (group, block_total * block) if last else (rows, width)
    outs = [pltpu.VMEM((shard_total // 2,) + part, bf16)] * 2
    if not first:
        outs.append(pltpu.VMEM(back.shape, bf16))
    if first:
        outs.append(pltpu.VMEM((rows, width), bf16))
        outs.append(pltpu.VMEM(held.shape, bf16))
    return pl.pallas_call(
        functools.partial(layer_kernel, turn, last, rows, unroll, shard_total, micro_count, own_count),
        out_shape=outs,
        in_specs=[ANY_SPEC] * 3
        + [VMEM_SPEC] * 2
        + [ANY_SPEC] * (3 * first)
        + [VMEM_SPEC] * (shard_total + (not first)),
        out_specs=[VMEM_SPEC] * len(outs),
        scratch_shapes=[
            pltpu.VMEM((block_total + 1, rows, block), bf16),
            pltpu.VMEM((blocks, rows, block), bf16),
            pltpu.VMEM((block_total + 1, rows, block), f32),
            pltpu.SMEM(lengths.shape, jnp.int32),
            pltpu.SMEM(in_index.shape, jnp.int32),
            pltpu.SMEM(out_index.shape, jnp.int32),
            pltpu.SemaphoreType.DMA((3,)),
        ]
        + ([pltpu.SemaphoreType.DMA((3, blocks))] if first else []),
        compiler_params=pltpu.CompilerParams(vmem_limit_bytes=vmem_limit(rows)),
        cost_estimate=pl.CostEstimate(
            flops=2 * rows * held.size, bytes_accessed=0, transcendentals=0
        ),
        input_output_aliases={4: 3} if first else {},
        name=f"layer_{turn}",
    )(lengths, in_index, out_index, gain, held, *(tiles if first else ()), *map(in_vmem, chunks), *(() if first else (in_vmem(back),)))


def pair_kernel(held_ref, even_ref, came_ref, own_ref, *send_refs):
    own_ref[...] = even_ref[0].astype(f32) + came_ref[0].astype(f32)
    for i, ref in enumerate(send_refs):
        ref[...] = (even_ref[i + 1].astype(f32) + came_ref[i + 1].astype(f32)).astype(bf16)


def pair_sum(held, even, came):
    parts, rows, width = even.shape
    return pl.pallas_call(
        pair_kernel,
        out_shape=[pltpu.VMEM((rows, width), f32)] + [pltpu.VMEM((rows, width), bf16)] * (parts - 1),
        in_specs=[VMEM_SPEC] * 3,
        out_specs=[VMEM_SPEC] * parts,
        compiler_params=pltpu.CompilerParams(vmem_limit_bytes=vmem_limit(rows)),
        name="pair_sum",
    )(held, in_vmem(even), in_vmem(came))


def finish_kernel(held_ref, x_ref, own_ref, *refs):
    sum_value = own_ref[...]
    for ref in refs[:-1]:
        sum_value = sum_value + ref[...].astype(f32)
    refs[-1][...] = (x_ref[...].astype(f32) + sum_value).astype(bf16)


def finish_sum(held, x_own, own, came):
    rows, width = x_own.shape
    return pl.pallas_call(
        finish_kernel,
        out_shape=pltpu.VMEM((rows, width), bf16),
        in_specs=[VMEM_SPEC] * (3 + len(came)),
        out_specs=VMEM_SPEC,
        compiler_params=pltpu.CompilerParams(vmem_limit_bytes=vmem_limit(rows)),
        name="finish_sum",
    )(held, *map(in_vmem, (x_own, own, *came)))


def result_kernel(last_turn, later_ref, x_ref, own_ref, *refs):
    out_ref = refs[-1]
    micro_count, own_count, _ = out_ref.shape
    sum_value = own_ref[...]
    for ref in refs[:-1]:
        sum_value = sum_value + ref[...].astype(f32)
    fresh = x_ref[...].astype(f32) + sum_value
    mine = lax.axis_index("section") == last_turn
    value = jnp.where(mine, fresh, later_ref[...].astype(f32))
    for m in range(micro_count):
        out_ref[m] = value[m * own_count : (m + 1) * own_count].astype(bf16)


def result_rows(last_turn, later, x_own, own, came, shape):
    return pl.pallas_call(
        functools.partial(result_kernel, last_turn),
        out_shape=jax.ShapeDtypeStruct(shape, bf16),
        in_specs=[VMEM_SPEC] * (3 + len(came)),
        out_specs=VMEM_SPEC,
        compiler_params=pltpu.CompilerParams(vmem_limit_bytes=vmem_limit(x_own.shape[0])),
        name="result_rows",
    )(*map(in_vmem, (later, x_own, own, *came)))


def body(tokens, lengths, norm_gain, gate_tiles, up_tiles, in_index, down_tiles, out_index):
    micro_count, own_count, model_width = tokens.shape
    block = gate_tiles.shape[-1]
    section_total = lax.axis_size("section")
    shard_total = lax.axis_size("shard")
    rows = live_total(tokens.shape, shard_total)
    gain = in_vmem(norm_gain.reshape(model_width // block, block))
    in_index, out_index = in_index[0], out_index[0]
    tiles = (gate_tiles[0], up_tiles[0], down_tiles[0])
    held = in_vmem(load_weights(*tiles[:2], rows))
    own_tokens = tokens.reshape(micro_count * own_count, model_width)
    came = same_core(own_tokens)[1:]
    chunks = both_cores([own_tokens, *relay(held, came, rows)])
    back = own_tokens
    for turn in range(section_total):
        first, last = turn == 0, turn + 1 == section_total
        parts = layer_step(
            turn, last, rows, lengths, in_index, out_index, gain, held, tiles, chunks, back, micro_count, own_count
        )
        if first:
            x_own, held = parts[2], in_vmem(parts[3])
        else:
            x_own, back = chunks[0], parts[2]
        sums = pair_sum(held, parts[0], xor_shard(parts[1], 1))
        came = [xor_shard(part, 2 * i + 2) for i, part in enumerate(sums[1:])]
        if not last:
            fresh = finish_sum(held, x_own, sums[0], came)
            chunks = both_cores(next_section(fresh, turn))
    later = lax.ppermute(back, "section", [(i + 1, i) for i in range(section_total - 1)])
    return result_rows(section_total - 1, later, back, sums[0], came, tokens.shape)[None]


def solution(mesh):
    placed = (
        P(None, "shard", None),
        P(),
        P("section", None),
        P("section", "shard", None, None, None),
        P("section", "shard", None, None, None),
        P("section", "shard", None),
        P("section", "shard", None, None, None),
        P("section", "shard", None),
    )
    return jax.shard_map(
        body,
        mesh=mesh,
        in_specs=placed,
        out_specs=P("section", None, "shard", None),
        check_vma=False,
    )
```
